32 devices in a mesh: lon: 8 (over z, core), lat: 4 (over y, x).
Axes of the slice: x: 2, y: 2, z: 4, core: 2. Of those that a mesh axis runs over, the one named last changes fastest.
Arguments:
- iterate: float32 [127, 4, 1024], P(None, 'lat', 'lon'), may hold values from -200 to 200
- residual: float32 [127, 4, 1024], P(None, 'lat', 'lon'), may hold values from -200 to 200
- direction: float32 [127, 4, 1024], P(None, 'lat', 'lon'), may hold values from -200 to 200
- obs_weight: float32 [127, 4, 1024], P(None, 'lat', 'lon'), may hold values from 0.5 to 5
- vertical: float32 [127, 127], replicated, may hold values from -0.2 to 1.2
- lon_taps: float32 [32, 101], replicated, may hold values from 0 to 1
- lat_taps: float32 [32, 101], replicated, may hold values from 0 to 1
- band_sizes: int32 [32], replicated, may hold values from 1 to 12, 127 in all
Outputs:
- iterate_next: float32 [127, 4, 1024], P(None, 'lat', 'lon')
- residual_next: float32 [127, 4, 1024], P(None, 'lat', 'lon')
- direction_next: float32 [127, 4, 1024], P(None, 'lat', 'lon')
The draws below stay inside these ranges and needn't reach their ends.
Inputs may be any that keep to these rules, and one draw needn't show every extreme that they name: `band_sizes`: the bands sum to 127 levels and the largest holds exactly 12 levels.
All inputs are finite; a program needn't handle non-finite values.
Results may differ from the reference program's by a relative error of at most 0.000071.
Values sent between devices are 32-bit elements; how exact they have to be, the bound alone decides.
A program may use at most 64 MiB of HBM per device.

```python
import math
import jax
import jax.numpy as jnp
import numpy as np
from jax import lax

LEV = 127
TAPS = 101
HALF = 50
GROUPS = 32
MOST = 12
NLAT = 4
NLON = 1024


def rough_field(key, salt):
    subkeys = jax.random.split(jax.random.fold_in(key, salt), 4)
    noise_part = jnp.clip(jax.random.normal(subkeys[0], (LEV, NLAT, NLON), jnp.float32), -6.0, 6.0)
    rise_rate = 0.5
    level_scale = jnp.exp(jax.random.uniform(subkeys[1], (LEV,), jnp.float32, math.log(0.3), math.log(3.0)))
    row_scale = jnp.exp(jax.random.uniform(subkeys[2], (NLAT,), jnp.float32, math.log(0.3), math.log(3.0)))
    column_scale = jnp.exp(jax.random.uniform(subkeys[3], (NLON,), jnp.float32, math.log(0.3), math.log(3.0)))
    row_trend = 3.0 ** (rise_rate * jnp.arange(NLAT, dtype=jnp.float32) / NLAT)
    column_trend = 3.0 ** (rise_rate * jnp.arange(NLON, dtype=jnp.float32) / NLON)
    rows = row_scale * row_trend
    columns = column_scale * column_trend
    return noise_part * level_scale[:, None, None] * rows[None, :, None] * columns[None, None, :] / 3.0


def smooth_kernel(key, salt):
    subkeys = jax.random.split(jax.random.fold_in(key, salt), 2)
    scales = jnp.exp(jax.random.uniform(subkeys[0], (GROUPS,), jnp.float32, math.log(2.0), math.log(40.0)))
    offsets = jnp.arange(TAPS, dtype=jnp.float32) - (TAPS - 1) // 2
    profile = jnp.exp(-offsets[None, :] ** 2 / (2.0 * scales[:, None] ** 2))
    profile = profile * jax.random.uniform(subkeys[1], (GROUPS, TAPS), jnp.float32, 0.5, 1.5)
    return profile / jnp.sqrt(jnp.sum(profile * profile, axis=1, keepdims=True))


def draw_iterate(key, part):
    return rough_field(key, 11)


def draw_residual(key, part):
    return rough_field(key, 12)


def draw_direction(key, part):
    return rough_field(key, 13)


def draw_vertical(key, part):
    subkey = jax.random.fold_in(key, 21)
    spread = jnp.clip(jax.random.normal(subkey, (LEV, LEV), jnp.float32), -4.0, 4.0)
    return jnp.eye(LEV, dtype=jnp.float32) + 0.5 * spread / math.sqrt(LEV)


def draw_lon_taps(key, part):
    return smooth_kernel(key, 31)


def draw_lat_taps(key, part):
    return smooth_kernel(key, 32)


def level_of(own_key, extent, pieces, smallest, high):
    factor_of, own = 1.0, jax.random.fold_in(own_key, 6)
    for position, blocks in pieces:
        draws = jnp.exp(jax.random.uniform(jax.random.fold_in(own, position), (blocks,), jnp.float32, smallest / len(pieces), high / len(pieces)))
        factor_of = factor_of * jnp.repeat(draws, extent[position] // blocks).reshape([-1 if axis == position else 1 for axis in range(len(extent))])
    return factor_of


def length_profile(amount, total, most, slope):
    loads = [(1 << 20) // math.isqrt(standing ** slope) + 1 for standing in range(2, amount + 1)]
    spare, holding = total - most - (amount - 1), [1] * (amount - 1)
    while spare > 0:
        candidates = [i for i in range(amount - 1) if holding[i] < most]
        pool, remaining = sum([loads[i] for i in candidates]), spare
        for i in candidates:
            addition = min(most - holding[i], max(1, remaining * loads[i] // pool), spare)
            holding[i] = holding[i] + addition
            spare = spare - addition
    return np.array([most] + holding)


def uneven(stream_key, count, total, most, lean):
    if count == 2:
        one = jax.random.randint(stream_key, (), max(1, total - most), min(most, total - 1) + 1)
        return jnp.stack([one, total - one])
    tallies = jnp.asarray(length_profile(count, total, most, lean), jnp.int32)
    twos = (count - 1) // 2
    giver, sink = tallies[1:1 + 2 * twos:2], tallies[2:2 + 2 * twos:2]
    slack = jnp.minimum(giver - 1, most - sink)
    moved = jax.random.randint(jax.random.fold_in(stream_key, 1), (twos,), 0, 1 << 20) % (slack + 1)
    tallies = tallies.at[1:1 + 2 * twos:2].set(giver - moved).at[2:2 + 2 * twos:2].set(sink + moved)
    return tallies[jax.random.permutation(jax.random.fold_in(stream_key, 2), count)]


def setup_inputs(seed: int = 0) -> dict:
    arg_keys = jax.random.split(jax.random.key(seed), 9)
    iterate = draw_iterate(jax.random.fold_in(arg_keys[8], 71), 0)
    residual = draw_residual(jax.random.fold_in(arg_keys[8], 71), 0)
    direction = draw_direction(jax.random.fold_in(arg_keys[8], 71), 0)
    obs_weight = jnp.clip(jnp.exp(math.log(5.0) - 2.3025851 * jax.random.uniform(arg_keys[3], (LEV, NLAT, NLON), jnp.float32) ** level_of(arg_keys[3], (LEV, NLAT, NLON), ((1, 4), (2, 8)), -0.2, 0.2)), 0.5, 5.0)
    vertical = draw_vertical(jax.random.fold_in(arg_keys[8], 71), 0)
    lon_taps = draw_lon_taps(jax.random.fold_in(arg_keys[8], 71), 0)
    lat_taps = draw_lat_taps(jax.random.fold_in(arg_keys[8], 71), 0)
    band_sizes = uneven(arg_keys[7], GROUPS, LEV, MOST, 2).astype(jnp.int32)
    return {"iterate": iterate, "residual": residual, "direction": direction, "obs_weight": obs_weight, "vertical": vertical, "lon_taps": lon_taps, "lat_taps": lat_taps, "band_sizes": band_sizes}


HIGHEST = lax.Precision.HIGHEST


def band_matrices(kernel, width_in, width_out, anchor):
    offsets = jnp.arange(width_in, dtype=jnp.int32)[:, None] - anchor - jnp.arange(width_out, dtype=jnp.int32)[None, :] + HALF
    inside = (offsets >= 0) & (offsets < TAPS)
    picked = kernel[:, jnp.clip(offsets, 0, TAPS - 1)]
    return jnp.where(inside[None], picked, jnp.zeros_like(picked))


def level_groups(band_sizes):
    bounds = jnp.cumsum(band_sizes).astype(jnp.int32)
    levels = jnp.arange(LEV, dtype=jnp.int32)
    return jnp.sum((levels[:, None] >= bounds[None, :]).astype(jnp.int32), axis=1).astype(jnp.int32)


def along_lon(grid_field, kernel):
    block_count = NLON // 128

    def single(level_pair):
        plane, level_kernel = level_pair
        blocks = plane.reshape(NLAT, block_count, 128)
        window = jnp.concatenate([jnp.roll(blocks, 1, axis=1), blocks, jnp.roll(blocks, -1, axis=1)], axis=2)
        matrix = band_matrices(level_kernel[None], 384, 128, 128)[0]
        return jnp.einsum("anc,co->ano", window, matrix, precision=HIGHEST).reshape(NLAT, NLON)

    return lax.map(single, (grid_field, kernel))


def along_lat(grid_field, kernel):
    def single(level_pair):
        plane, level_kernel = level_pair
        matrix = band_matrices(level_kernel[None], NLAT, NLAT, 0)[0]
        return jnp.einsum("ca,cx->ax", matrix, plane, precision=HIGHEST)

    return lax.map(single, (grid_field, kernel))


def vertical_mix(matrix, grid_field):
    return jnp.dot(matrix, grid_field.reshape(LEV, -1), precision=HIGHEST).reshape(grid_field.shape)


def reference(iterate, residual, direction, obs_weight, vertical, lon_taps, lat_taps, band_sizes):
    groups = level_groups(band_sizes)
    lon_rows = lon_taps[groups]
    lat_rows = lat_taps[groups]
    lon_part = along_lon(direction, lon_rows)
    lat_part = along_lat(lon_part, lat_rows)
    lifted = vertical_mix(vertical, lat_part)
    weighted = obs_weight * lifted
    back_vert = vertical_mix(vertical.T, weighted)
    back_lat = along_lat(back_vert, lat_rows[:, ::-1])
    image = direction + along_lon(back_lat, lon_rows[:, ::-1])
    norm_old = jnp.sum(residual * residual)
    curvature = jnp.sum(direction * image)
    alpha = norm_old / curvature
    iterate_next = iterate + alpha * direction
    residual_next = residual - alpha * image
    norm_new = jnp.sum(residual_next * residual_next)
    direction_next = residual_next + (norm_new / norm_old) * direction
    return iterate_next, residual_next, direction_next
```

```python
import functools

import jax
import jax.numpy as jnp
from jax import lax
from jax.experimental import pallas as pl
from jax.experimental.pallas import tpu as pltpu
from jax.sharding import PartitionSpec as P

LEV = 127
PADDED = 128
TAPS = 101
HALF = 50
GROUPS = 32
LANES = 128
SIDE = LANES // 2
FIRST = SIDE - HALF
STRIDE = 8
HIGHEST = lax.Precision.HIGHEST
MESH = pl.DeviceIdType.MESH
OWN, LEFT, RIGHT = 0, 1, 2


def shifted(low, high, lane, amount):
    if amount == 0:
        return low
    return jnp.where(
        lane < LANES - amount,
        pltpu.roll(low, LANES - amount, 1),
        pltpu.roll(high, LANES - amount, 1),
    )


def kernel(
    n_lon,
    n_lat,
    iterate_ref,
    residual_ref,
    direction_ref,
    weight_ref,
    vertical_ref,
    lon_taps_ref,
    lat_taps_ref,
    sizes_ref,
    iterate_out,
    residual_out,
    direction_out,
    held_d,
    held_r,
    held_b,
    matrix,
    flipped,
    gathered,
    gathered_r,
    window,
    lon_coef,
    lat_coef,
    filtered,
    image_part,
    lat_part,
    image,
    sums,
    sums_lat,
    sums_row,
    sums_lon,
    send_sem,
    recv_sem,
    back_send,
    back_recv,
    lat_send,
    lat_recv,
    lon_send,
    lon_recv,
):
    chunk = PADDED // n_lat
    tiles = chunk // 8
    my_lon, my_lat = lax.axis_index("lon"), lax.axis_index("lat")
    left = lax.rem(my_lon + n_lon - 1, n_lon)
    right = lax.rem(my_lon + 1, n_lon)

    def lat_at(step):
        return lax.rem(my_lat + step, n_lat)

    def rows_of(index):
        return pl.ds(pl.multiple_of(index * chunk, chunk), chunk)

    barrier = pltpu.get_barrier_semaphore()
    greeted = 0
    for step in range(n_lat):
        for lon in (my_lon, left, right):
            if step == 0 and lon is my_lon:
                continue
            pl.semaphore_signal(
                barrier, inc=1, device_id=(lon, lat_at(step)), device_id_type=MESH
            )
            greeted += 1
    for step in range(2, n_lon - 1):
        pl.semaphore_signal(
            barrier,
            inc=1,
            device_id=(lax.rem(my_lon + step, n_lon), my_lat),
            device_id_type=MESH,
        )
        greeted += 1

    held_d[pl.ds(PADDED - 8, 8), :] = jnp.zeros((8, LANES), jnp.float32)
    held_r[pl.ds(PADDED - 8, 8), :] = jnp.zeros((8, LANES), jnp.float32)
    held_d[pl.ds(0, LEV), :] = direction_ref[...]
    held_r[pl.ds(0, LEV), :] = residual_ref[...]

    pl.semaphore_wait(barrier, greeted)

    def send_block(held, phase, kind, step):
        to = lat_at(step)
        lon = (my_lon, left, right)[kind]
        slot = (OWN, RIGHT, LEFT)[kind]
        copy = pltpu.make_async_remote_copy(
            src_ref=held.at[rows_of(to), :],
            dst_ref=gathered.at[phase, slot, my_lat],
            send_sem=send_sem.at[phase, slot, to],
            recv_sem=recv_sem.at[phase, slot, my_lat],
            device_id=(lon, to),
            device_id_type=MESH,
        )
        copy.start()
        return copy

    def send_residual(step):
        to = lat_at(step)
        copy = pltpu.make_async_remote_copy(
            src_ref=held_r.at[rows_of(to), :],
            dst_ref=gathered_r.at[my_lat],
            send_sem=send_sem.at[0, 3, to],
            recv_sem=recv_sem.at[0, 3, my_lat],
            device_id=(my_lon, to),
            device_id_type=MESH,
        )
        copy.start()
        return copy

    def arrived(phase, kind, step):
        source = lat_at(step)
        place = gathered_r.at[source] if kind == 3 else gathered.at[phase, kind, source]
        pltpu.make_async_remote_copy(
            src_ref=place,
            dst_ref=place,
            send_sem=send_sem.at[phase, kind, source],
            recv_sem=recv_sem.at[phase, kind, source],
            device_id=(my_lon, source),
            device_id_type=MESH,
        ).wait_recv()

    def send_all(held, phase):
        copies = []
        for step in list(range(1, n_lat)) + [0]:
            for kind in (LEFT, RIGHT, OWN):
                if step or kind:
                    copies.append(send_block(held, phase, kind, step))
        gathered[phase, OWN, my_lat] = held[rows_of(my_lat), :]
        return copies

    def await_all(phase):
        for step in range(n_lat):
            for kind in (OWN, LEFT, RIGHT):
                if step or kind:
                    arrived(phase, kind, step)

    def send_back(parts, whole, phase):
        copies = []
        for step in range(1, n_lat):
            to = lat_at(step)
            copy = pltpu.make_async_remote_copy(
                src_ref=parts.at[to],
                dst_ref=whole.at[rows_of(my_lat), :],
                send_sem=back_send.at[phase, to],
                recv_sem=back_recv.at[phase, my_lat],
                device_id=(my_lon, to),
                device_id_type=MESH,
            )
            copy.start()
            copies.append(copy)
        whole[rows_of(my_lat), :] = parts[my_lat]
        return copies

    def await_back(whole, phase):
        for step in range(1, n_lat):
            source = lat_at(step)
            place = whole.at[rows_of(source), :]
            pltpu.make_async_remote_copy(
                src_ref=place,
                dst_ref=place,
                send_sem=back_send.at[phase, source],
                recv_sem=back_recv.at[phase, source],
                device_id=(my_lon, source),
                device_id_type=MESH,
            ).wait_recv()

    pending = send_all(held_d, 0)
    pending += [send_residual(step) for step in range(1, n_lat)]
    gathered_r[my_lat] = held_r[rows_of(my_lat), :]

    upto = (
        lax.broadcasted_iota(jnp.int32, (GROUPS, GROUPS), 0)
        <= lax.broadcasted_iota(jnp.int32, (GROUPS, GROUPS), 1)
    ).astype(jnp.float32)
    sizes = jnp.broadcast_to(sizes_ref[...].astype(jnp.float32), (8, GROUPS))
    bounds = jnp.dot(sizes, upto, precision=HIGHEST)[0:1, :]
    starts = bounds - sizes[0:1, :]
    level = (
        lax.broadcasted_iota(jnp.int32, (chunk, GROUPS), 0) + my_lat * chunk
    ).astype(jnp.float32)
    member = ((level > starts - 0.5) & (level < bounds - 0.5)).astype(jnp.float32)
    lon_rows = jnp.dot(member, lon_taps_ref[...], precision=HIGHEST)
    lat_rows = jnp.dot(member, lat_taps_ref[...], precision=HIGHEST)
    for tap in range(TAPS):
        lon_coef[tap] = jnp.broadcast_to(lon_rows[:, tap : tap + 1], (chunk, LANES))
    for offset in range(2 * n_lat - 1):
        tap = HALF - (n_lat - 1) + offset
        if 0 <= tap < TAPS:
            lat_coef[offset] = jnp.broadcast_to(lat_rows[:, tap : tap + 1], (chunk, LANES))
        else:
            lat_coef[offset] = jnp.zeros((chunk, LANES), jnp.float32)

    matrix[...] = jnp.zeros_like(matrix)
    matrix[pl.ds(0, LEV), pl.ds(0, LEV)] = vertical_ref[...]
    flipped[...] = matrix[...].T

    lane = lax.broadcasted_iota(jnp.int32, (8, LANES), 1)

    def filter_chunk(phase, adjoint, finish):
        def widen(at, _):
            row = pl.ds(pl.multiple_of(at * 8, 8), 8)
            for lat in range(n_lat):
                mine = pltpu.roll(gathered[phase, OWN, lat, row, :], SIDE, 1)
                before = pltpu.roll(gathered[phase, LEFT, lat, row, :], SIDE, 1)
                after = pltpu.roll(gathered[phase, RIGHT, lat, row, :], SIDE, 1)
                window[lat, 0, row, :] = jnp.where(lane < SIDE, before, mine)
                window[lat, 1, row, :] = jnp.where(lane < SIDE, mine, after)
            return 0

        lax.fori_loop(0, tiles, widen, 0)

        def one(at, _):
            out_lat = at // tiles
            row = pl.ds(pl.multiple_of(lax.rem(at, tiles) * 8, 8), 8)
            low = jnp.zeros((8, LANES), jnp.float32)
            high = jnp.zeros((8, LANES), jnp.float32)
            for lat in range(n_lat):
                offset = out_lat - lat if adjoint else lat - out_lat
                scale = lat_coef[offset + n_lat - 1, row, :]
                low = low + scale * window[lat, 0, row, :]
                high = high + scale * window[lat, 1, row, :]
            lows = [shifted(low, high, lane, j) for j in range(STRIDE)]
            highs = [shifted(high, low, lane, j) for j in range(STRIDE)]
            total = jnp.zeros((8, LANES), jnp.float32)
            for base in range(0, TAPS, STRIDE):
                part_low = part_high = None
                for j in range(min(STRIDE, TAPS - base)):
                    tap = base + j
                    scale = lon_coef[TAPS - 1 - tap if adjoint else tap, row, :]
                    if part_low is None:
                        part_low, part_high = scale * lows[j], scale * highs[j]
                    else:
                        part_low = part_low + scale * lows[j]
                        part_high = part_high + scale * highs[j]
                total = total + shifted(part_low, part_high, lane, FIRST + base)
            finish(out_lat, row, total)
            return 0

        lax.fori_loop(0, n_lat * tiles, one, 0)

    await_all(0)

    def keep(out_lat, row, total):
        filtered[out_lat, row, :] = total

    filter_chunk(0, False, keep)
    pending += send_back(filtered, lat_part, 0)
    await_back(lat_part, 0)

    lifted = jnp.dot(matrix[...], lat_part[...], precision=HIGHEST)
    held_b[...] = lifted
    held_b[pl.ds(0, LEV), :] = held_b[pl.ds(0, LEV), :] * weight_ref[...]
    held_b[...] = jnp.dot(flipped[...], held_b[...], precision=HIGHEST)

    pending += send_all(held_b, 1)
    for step in range(1, n_lat):
        arrived(0, 3, step)
    await_all(1)

    sums[...] = jnp.zeros_like(sums)

    def add(out_lat, row, total):
        total = total + gathered[0, OWN, out_lat, row, :]
        image_part[out_lat, row, :] = total
        old = gathered_r[out_lat, row, :]
        sums[0] += old * old
        sums[1] += total * gathered[0, OWN, out_lat, row, :]
        sums[2] += total * old
        sums[3] += total * total

    filter_chunk(1, True, add)
    pending += send_back(image_part, image, 1)

    def exchange(slots, send, recv, mine, count, to_device):
        copies = []
        for step in range(1, count):
            to = lax.rem(mine + step, count)
            copy = pltpu.make_async_remote_copy(
                src_ref=slots.at[mine],
                dst_ref=slots.at[mine],
                send_sem=send.at[to],
                recv_sem=recv.at[mine],
                device_id=to_device(to),
                device_id_type=MESH,
            )
            copy.start()
            copies.append(copy)
        for step in range(1, count):
            source = lax.rem(mine + step, count)
            pltpu.make_async_remote_copy(
                src_ref=slots.at[source],
                dst_ref=slots.at[source],
                send_sem=send.at[source],
                recv_sem=recv.at[source],
                device_id=to_device(source),
                device_id_type=MESH,
            ).wait_recv()
        total = slots[0]
        for index in range(1, count):
            total = total + slots[index]
        return total, copies

    rows = [jnp.sum(sums[i], axis=0, keepdims=True) for i in range(4)]
    sums_lat[my_lat] = jnp.concatenate(rows + [jnp.zeros((4, LANES), jnp.float32)], axis=0)
    total, copies = exchange(
        sums_lat, lat_send, lat_recv, my_lat, n_lat, lambda to: (my_lon, to)
    )
    pending += copies
    sums_lon[my_lon] = total
    total, copies = exchange(
        sums_lon, lon_send, lon_recv, my_lon, n_lon, lambda to: (to, my_lat)
    )
    pending += copies
    await_back(image, 1)

    total = jnp.sum(total, axis=1, keepdims=True)
    norm_old, curvature = total[0:1, :], total[1:2, :]
    crossed, squared = total[2:3, :], total[3:4, :]
    alpha = norm_old / curvature
    norm_new = norm_old - 2.0 * alpha * crossed + alpha * alpha * squared
    ratio = norm_new / norm_old
    direction = direction_ref[...]
    residual_next = residual_ref[...] - alpha * image[pl.ds(0, LEV), :]
    iterate_out[...] = iterate_ref[...] + alpha * direction
    residual_out[...] = residual_next
    direction_out[...] = residual_next + ratio * direction

    for copy in pending:
        copy.wait_send()


def local(n_lon, n_lat, iterate, residual, direction, obs_weight, vertical, lon_taps, lat_taps, band_sizes):
    chunk = PADDED // n_lat
    flat = [x.reshape(LEV, LANES) for x in (iterate, residual, direction, obs_weight)]
    f32 = jnp.float32
    vmem = pl.BlockSpec(memory_space=pltpu.VMEM)
    outs = pl.pallas_call(
        functools.partial(kernel, n_lon, n_lat),
        out_shape=[jax.ShapeDtypeStruct((LEV, LANES), f32)] * 3,
        in_specs=[vmem] * 8,
        out_specs=[vmem] * 3,
        scratch_shapes=[
            pltpu.VMEM((PADDED, LANES), f32),
            pltpu.VMEM((PADDED, LANES), f32),
            pltpu.VMEM((PADDED, LANES), f32),
            pltpu.VMEM((PADDED, PADDED), f32),
            pltpu.VMEM((PADDED, PADDED), f32),
            pltpu.VMEM((2, 3, n_lat, chunk, LANES), f32),
            pltpu.VMEM((n_lat, chunk, LANES), f32),
            pltpu.VMEM((n_lat, 2, chunk, LANES), f32),
            pltpu.VMEM((TAPS, chunk, LANES), f32),
            pltpu.VMEM((2 * n_lat - 1, chunk, LANES), f32),
            pltpu.VMEM((n_lat, chunk, LANES), f32),
            pltpu.VMEM((n_lat, chunk, LANES), f32),
            pltpu.VMEM((PADDED, LANES), f32),
            pltpu.VMEM((PADDED, LANES), f32),
            pltpu.VMEM((4, 8, LANES), f32),
            pltpu.VMEM((n_lat, 8, LANES), f32),
            pltpu.VMEM((8, LANES), f32),
            pltpu.VMEM((n_lon, 8, LANES), f32),
            pltpu.SemaphoreType.DMA((2, 4, n_lat)),
            pltpu.SemaphoreType.DMA((2, 4, n_lat)),
            pltpu.SemaphoreType.DMA((2, n_lat)),
            pltpu.SemaphoreType.DMA((2, n_lat)),
            pltpu.SemaphoreType.DMA((n_lat,)),
            pltpu.SemaphoreType.DMA((n_lat,)),
            pltpu.SemaphoreType.DMA((n_lon,)),
            pltpu.SemaphoreType.DMA((n_lon,)),
        ],
        compiler_params=pltpu.CompilerParams(
            collective_id=0,
            has_side_effects=True,
            vmem_limit_bytes=32 * 1024 * 1024,
        ),
    )(*flat, vertical, lon_taps, lat_taps, band_sizes.reshape(1, GROUPS))
    return tuple(x.reshape(LEV, 1, LANES) for x in outs)


def solution(mesh):
    field = P(None, "lat", "lon")
    return jax.shard_map(
        functools.partial(local, mesh.shape["lon"], mesh.shape["lat"]),
        mesh=mesh,
        in_specs=(field,) * 4 + (P(),) * 4,
        out_specs=(field,) * 3,
        check_vma=False,
    )
```

```python
import functools

import jax
import jax.numpy as jnp
from jax import lax
from jax.experimental import pallas as pl
from jax.experimental.pallas import tpu as pltpu
from jax.sharding import PartitionSpec as P

LEV = 127
PADDED = 128
TAPS = 101
HALF = 50
GROUPS = 32
LANES = 128
SIDE = LANES // 2
FIRST = SIDE - HALF
STRIDE = 8
TOGETHER = 4
HIGHEST = lax.Precision.HIGHEST
MESH = pl.DeviceIdType.MESH
OWN, LEFT, RIGHT = 0, 1, 2


def shifted(low, high, lane, amount):
    if amount == 0:
        return low
    return jnp.where(
        lane < LANES - amount,
        pltpu.roll(low, LANES - amount, 1),
        pltpu.roll(high, LANES - amount, 1),
    )


def kernel(
    n_lon,
    n_lat,
    iterate_hbm,
    residual_hbm,
    direction_hbm,
    weight_hbm,
    vertical_hbm,
    lon_taps_hbm,
    lat_taps_hbm,
    sizes_hbm,
    iterate_out,
    residual_out,
    direction_out,
    held_i,
    held_w,
    vertical_ref,
    lon_taps_ref,
    lat_taps_ref,
    sizes_ref,
    nexts,
    load_sem,
    store_sem,
    held_d,
    held_r,
    held_b,
    matrix,
    flipped,
    gathered,
    gathered_r,
    window,
    shifts,
    lon_coef,
    lat_coef,
    filtered,
    image_part,
    lat_part,
    image,
    sums,
    sums_lat,
    sums_all,
    send_sem,
    recv_sem,
    back_send,
    back_recv,
    lat_send,
    lat_recv,
    lon_send,
    lon_recv,
):
    chunk = PADDED // n_lat
    tiles = chunk // 8
    direct = n_lon * n_lat <= 64
    my_lon, my_lat = lax.axis_index("lon"), lax.axis_index("lat")
    left = lax.rem(my_lon + n_lon - 1, n_lon)
    right = lax.rem(my_lon + 1, n_lon)

    def lat_at(step):
        return lax.rem(my_lat + step, n_lat)

    def rows_of(index):
        return pl.ds(pl.multiple_of(index * chunk, chunk), chunk)

    def load(source, place, index):
        copy = pltpu.make_async_copy(source, place, load_sem.at[index])
        copy.start()
        return copy

    levels = pl.ds(0, LEV)
    loads = [
        load(direction_hbm.at[:, 0, :], held_d.at[levels, :], 0),
        load(residual_hbm.at[:, 0, :], held_r.at[levels, :], 1),
        load(sizes_hbm, sizes_ref, 2),
        load(lon_taps_hbm, lon_taps_ref, 3),
        load(lat_taps_hbm, lat_taps_ref, 4),
        load(vertical_hbm, vertical_ref, 5),
        load(weight_hbm.at[:, 0, :], held_w.at[levels, :], 6),
        load(iterate_hbm.at[:, 0, :], held_i.at[levels, :], 7),
    ]

    barrier = pltpu.get_barrier_semaphore()
    greeted = 0
    for step in range(n_lat):
        for lon in (my_lon, left, right):
            if step == 0 and lon is my_lon:
                continue
            pl.semaphore_signal(
                barrier, inc=1, device_id=(lon, lat_at(step)), device_id_type=MESH
            )
            greeted += 1
    for across in range(n_lat if direct else 1):
        for step in range(2, n_lon - 1):
            pl.semaphore_signal(
                barrier,
                inc=1,
                device_id=(lax.rem(my_lon + step, n_lon), lat_at(across)),
                device_id_type=MESH,
            )
            greeted += 1

    held_d[pl.ds(LEV, 1), :] = jnp.zeros((1, LANES), jnp.float32)
    held_r[pl.ds(LEV, 1), :] = jnp.zeros((1, LANES), jnp.float32)
    loads[0].wait()
    loads[1].wait()

    pl.semaphore_wait(barrier, greeted)

    def send_block(held, phase, kind, step):
        to = lat_at(step)
        lon = (my_lon, left, right)[kind]
        slot = (OWN, RIGHT, LEFT)[kind]
        copy = pltpu.make_async_remote_copy(
            src_ref=held.at[rows_of(to), :],
            dst_ref=gathered.at[phase, slot, my_lat],
            send_sem=send_sem.at[phase, slot, to],
            recv_sem=recv_sem.at[phase, slot, my_lat],
            device_id=(lon, to),
            device_id_type=MESH,
        )
        copy.start()
        return copy

    def send_residual(step):
        to = lat_at(step)
        copy = pltpu.make_async_remote_copy(
            src_ref=held_r.at[rows_of(to), :],
            dst_ref=gathered_r.at[my_lat],
            send_sem=send_sem.at[0, 3, to],
            recv_sem=recv_sem.at[0, 3, my_lat],
            device_id=(my_lon, to),
            device_id_type=MESH,
        )
        copy.start()
        return copy

    def arrived(phase, kind, step):
        source = lat_at(step)
        place = gathered_r.at[source] if kind == 3 else gathered.at[phase, kind, source]
        pltpu.make_async_remote_copy(
            src_ref=place,
            dst_ref=place,
            send_sem=send_sem.at[phase, kind, source],
            recv_sem=recv_sem.at[phase, kind, source],
            device_id=(my_lon, source),
            device_id_type=MESH,
        ).wait_recv()

    def send_all(held, phase):
        copies = []
        for step in list(range(1, n_lat)) + [0]:
            for kind in (LEFT, RIGHT, OWN):
                if step or kind:
                    copies.append(send_block(held, phase, kind, step))
        gathered[phase, OWN, my_lat] = held[rows_of(my_lat), :]
        return copies

    def await_all(phase):
        for step in range(n_lat):
            for kind in (OWN, LEFT, RIGHT):
                if step or kind:
                    arrived(phase, kind, step)

    def send_back(parts, whole, phase):
        copies = []
        for step in range(1, n_lat):
            to = lat_at(step)
            copy = pltpu.make_async_remote_copy(
                src_ref=parts.at[to],
                dst_ref=whole.at[rows_of(my_lat), :],
                send_sem=back_send.at[phase, to],
                recv_sem=back_recv.at[phase, my_lat],
                device_id=(my_lon, to),
                device_id_type=MESH,
            )
            copy.start()
            copies.append(copy)
        whole[rows_of(my_lat), :] = parts[my_lat]
        return copies

    def await_back(whole, phase):
        for step in range(1, n_lat):
            source = lat_at(step)
            place = whole.at[rows_of(source), :]
            pltpu.make_async_remote_copy(
                src_ref=place,
                dst_ref=place,
                send_sem=back_send.at[phase, source],
                recv_sem=back_recv.at[phase, source],
                device_id=(my_lon, source),
                device_id_type=MESH,
            ).wait_recv()

    pending = send_all(held_d, 0)
    pending += [send_residual(step) for step in range(1, n_lat)]
    gathered_r[my_lat] = held_r[rows_of(my_lat), :]

    for copy in loads[2:6]:
        copy.wait()

    upto = (
        lax.broadcasted_iota(jnp.int32, (GROUPS, GROUPS), 0)
        <= lax.broadcasted_iota(jnp.int32, (GROUPS, GROUPS), 1)
    ).astype(jnp.float32)
    sizes = jnp.broadcast_to(sizes_ref[...].astype(jnp.float32), (8, GROUPS))
    bounds = jnp.dot(sizes, upto, precision=HIGHEST)[0:1, :]
    starts = bounds - sizes[0:1, :]
    level = (
        lax.broadcasted_iota(jnp.int32, (chunk, GROUPS), 0) + my_lat * chunk
    ).astype(jnp.float32)
    member = ((level > starts - 0.5) & (level < bounds - 0.5)).astype(jnp.float32)
    lon_rows = jnp.dot(member, lon_taps_ref[...], precision=HIGHEST)
    lat_rows = jnp.dot(member, lat_taps_ref[...], precision=HIGHEST)
    for tap in range(TAPS):
        lon_coef[tap] = jnp.broadcast_to(lon_rows[:, tap : tap + 1], (chunk, LANES))
    for offset in range(2 * n_lat - 1):
        tap = HALF - (n_lat - 1) + offset
        if 0 <= tap < TAPS:
            lat_coef[offset] = jnp.broadcast_to(lat_rows[:, tap : tap + 1], (chunk, LANES))
        else:
            lat_coef[offset] = jnp.zeros((chunk, LANES), jnp.float32)

    matrix[...] = jnp.zeros_like(matrix)
    matrix[pl.ds(0, LEV), pl.ds(0, LEV)] = vertical_ref[...]
    flipped[...] = matrix[...].T

    lane = lax.broadcasted_iota(jnp.int32, (8, LANES), 1)

    def filter_chunk(phase, adjoint, finish):
        for at in range(tiles):
            row = pl.ds(at * 8, 8)
            for lat in range(n_lat):
                mine = pltpu.roll(gathered[phase, OWN, lat, row, :], SIDE, 1)
                before = pltpu.roll(gathered[phase, LEFT, lat, row, :], SIDE, 1)
                after = pltpu.roll(gathered[phase, RIGHT, lat, row, :], SIDE, 1)
                window[lat, 0, row, :] = jnp.where(lane < SIDE, before, mine)
                window[lat, 1, row, :] = jnp.where(lane < SIDE, mine, after)

        def some(at, _):
            first = lax.rem(at, n_lat // TOGETHER) * TOGETHER
            row = pl.ds(pl.multiple_of(at // (n_lat // TOGETHER) * 8, 8), 8)
            for out in range(TOGETHER):
                low = jnp.zeros((8, LANES), jnp.float32)
                high = jnp.zeros((8, LANES), jnp.float32)
                for lat in range(n_lat):
                    offset = first + (out - lat) if adjoint else lat - out - first
                    scale = lat_coef[offset + n_lat - 1, row, :]
                    low = low + scale * window[lat, 0, row, :]
                    high = high + scale * window[lat, 1, row, :]
                for j in range(STRIDE):
                    shifts[out, 0, j] = shifted(low, high, lane, j)
                    shifts[out, 1, j] = shifted(high, low, lane, j)
            totals = [jnp.zeros((8, LANES), jnp.float32)] * TOGETHER
            for base in range(0, TAPS, STRIDE):
                parts = [None] * TOGETHER
                for j in range(min(STRIDE, TAPS - base)):
                    tap = base + j
                    scale = lon_coef[TAPS - 1 - tap if adjoint else tap, row, :]
                    for out in range(TOGETHER):
                        low, high = scale * shifts[out, 0, j], scale * shifts[out, 1, j]
                        if parts[out] is not None:
                            low, high = parts[out][0] + low, parts[out][1] + high
                        parts[out] = low, high
                for out in range(TOGETHER):
                    totals[out] = totals[out] + shifted(*parts[out], lane, FIRST + base)
            for out in range(TOGETHER):
                finish(first + out, row, totals[out])
            return 0

        lax.fori_loop(0, tiles * (n_lat // TOGETHER), some, 0)

    loads[6].wait()
    loads[7].wait()
    await_all(0)

    def keep(out_lat, row, total):
        filtered[out_lat, row, :] = total

    filter_chunk(0, False, keep)
    pending += send_back(filtered, lat_part, 0)
    await_back(lat_part, 0)

    lifted = jnp.dot(matrix[...], lat_part[...], precision=HIGHEST)
    held_b[...] = lifted
    held_b[pl.ds(0, LEV), :] = held_b[pl.ds(0, LEV), :] * held_w[levels, :]
    held_b[...] = jnp.dot(flipped[...], held_b[...], precision=HIGHEST)

    pending += send_all(held_b, 1)
    for step in range(1, n_lat):
        arrived(0, 3, step)
    await_all(1)

    sums[...] = jnp.zeros_like(sums)

    def add(out_lat, row, total):
        total = total + gathered[0, OWN, out_lat, row, :]
        image_part[out_lat, row, :] = total
        old = gathered_r[out_lat, row, :]
        sums[0] += old * old
        sums[1] += total * gathered[0, OWN, out_lat, row, :]
        sums[2] += total * old
        sums[3] += total * total

    filter_chunk(1, True, add)
    pending += send_back(image_part, image, 1)

    def exchange(slots, send, recv, mine, count, to_device):
        copies = []
        for step in range(1, count):
            to = lax.rem(mine + step, count)
            copy = pltpu.make_async_remote_copy(
                src_ref=slots.at[mine],
                dst_ref=slots.at[mine],
                send_sem=send.at[to],
                recv_sem=recv.at[mine],
                device_id=to_device(to),
                device_id_type=MESH,
            )
            copy.start()
            copies.append(copy)
        for step in range(1, count):
            source = lax.rem(mine + step, count)
            pltpu.make_async_remote_copy(
                src_ref=slots.at[source],
                dst_ref=slots.at[source],
                send_sem=send.at[source],
                recv_sem=recv.at[source],
                device_id=to_device(source),
                device_id_type=MESH,
            ).wait_recv()
        total = slots[0]
        for index in range(1, count):
            total = total + slots[index]
        return total, copies

    rows = [jnp.sum(sums[i], axis=0, keepdims=True) for i in range(4)]
    mine = jnp.concatenate(rows + [jnp.zeros((4, LANES), jnp.float32)], axis=0)
    if direct:
        me = my_lon * n_lat + my_lat
        sums_all[me] = mine
        total, copies = exchange(
            sums_all,
            lon_send,
            lon_recv,
            me,
            n_lon * n_lat,
            lambda to: (to // n_lat, lax.rem(to, n_lat)),
        )
        pending += copies
    else:
        sums_lat[my_lat] = mine
        total, copies = exchange(
            sums_lat, lat_send, lat_recv, my_lat, n_lat, lambda to: (my_lon, to)
        )
        pending += copies
        sums_all[my_lon] = total
        total, copies = exchange(
            sums_all, lon_send, lon_recv, my_lon, n_lon, lambda to: (to, my_lat)
        )
        pending += copies
    await_back(image, 1)

    total = jnp.sum(total, axis=1, keepdims=True)
    norm_old, curvature = total[0:1, :], total[1:2, :]
    crossed, squared = total[2:3, :], total[3:4, :]
    alpha = norm_old / curvature
    norm_new = norm_old - 2.0 * alpha * crossed + alpha * alpha * squared
    ratio = norm_new / norm_old
    direction = held_d[levels, :]
    residual_next = held_r[levels, :] - alpha * image[levels, :]
    nexts[0, levels, :] = held_i[levels, :] + alpha * direction
    nexts[1, levels, :] = residual_next
    nexts[2, levels, :] = residual_next + ratio * direction
    stores = []
    for index, out in enumerate((iterate_out, residual_out, direction_out)):
        copy = pltpu.make_async_copy(
            nexts.at[index, levels, :], out.at[:, 0, :], store_sem.at[index]
        )
        copy.start()
        stores.append(copy)

    for copy in pending:
        copy.wait_send()
    for copy in stores:
        copy.wait()


def local(n_lon, n_lat, iterate, residual, direction, obs_weight, vertical, lon_taps, lat_taps, band_sizes):
    chunk = PADDED // n_lat
    last = n_lon * n_lat if n_lon * n_lat <= 64 else n_lon
    f32 = jnp.float32
    hbm = pl.BlockSpec(memory_space=pltpu.HBM)
    return pl.pallas_call(
        functools.partial(kernel, n_lon, n_lat),
        out_shape=[jax.ShapeDtypeStruct((LEV, 1, LANES), f32)] * 3,
        in_specs=[hbm] * 8,
        out_specs=[hbm] * 3,
        scratch_shapes=[
            pltpu.VMEM((PADDED, LANES), f32),
            pltpu.VMEM((PADDED, LANES), f32),
            pltpu.VMEM((LEV, LEV), f32),
            pltpu.VMEM((GROUPS, TAPS), f32),
            pltpu.VMEM((GROUPS, TAPS), f32),
            pltpu.VMEM((1, GROUPS), jnp.int32),
            pltpu.VMEM((3, PADDED, LANES), f32),
            pltpu.SemaphoreType.DMA((8,)),
            pltpu.SemaphoreType.DMA((3,)),
            pltpu.VMEM((PADDED, LANES), f32),
            pltpu.VMEM((PADDED, LANES), f32),
            pltpu.VMEM((PADDED, LANES), f32),
            pltpu.VMEM((PADDED, PADDED), f32),
            pltpu.VMEM((PADDED, PADDED), f32),
            pltpu.VMEM((2, 3, n_lat, chunk, LANES), f32),
            pltpu.VMEM((n_lat, chunk, LANES), f32),
            pltpu.VMEM((n_lat, 2, chunk, LANES), f32),
            pltpu.VMEM((TOGETHER, 2, STRIDE, 8, LANES), f32),
            pltpu.VMEM((TAPS, chunk, LANES), f32),
            pltpu.VMEM((2 * n_lat - 1, chunk, LANES), f32),
            pltpu.VMEM((n_lat, chunk, LANES), f32),
            pltpu.VMEM((n_lat, chunk, LANES), f32),
            pltpu.VMEM((PADDED, LANES), f32),
            pltpu.VMEM((PADDED, LANES), f32),
            pltpu.VMEM((4, 8, LANES), f32),
            pltpu.VMEM((n_lat, 8, LANES), f32),
            pltpu.VMEM((last, 8, LANES), f32),
            pltpu.SemaphoreType.DMA((2, 4, n_lat)),
            pltpu.SemaphoreType.DMA((2, 4, n_lat)),
            pltpu.SemaphoreType.DMA((2, n_lat)),
            pltpu.SemaphoreType.DMA((2, n_lat)),
            pltpu.SemaphoreType.DMA((n_lat,)),
            pltpu.SemaphoreType.DMA((n_lat,)),
            pltpu.SemaphoreType.DMA((last,)),
            pltpu.SemaphoreType.DMA((last,)),
        ],
        compiler_params=pltpu.CompilerParams(
            collective_id=0,
            has_side_effects=True,
            vmem_limit_bytes=64 * 1024 * 1024,
        ),
    )(
        iterate,
        residual,
        direction,
        obs_weight,
        vertical,
        lon_taps,
        lat_taps,
        band_sizes.reshape(1, GROUPS),
    )


def solution(mesh):
    field = P(None, "lat", "lon")
    return jax.shard_map(
        functools.partial(local, mesh.shape["lon"], mesh.shape["lat"]),
        mesh=mesh,
        in_specs=(field,) * 4 + (P(),) * 4,
        out_specs=(field,) * 3,
        check_vma=False,
    )
```

```python
import functools

import jax
import jax.numpy as jnp
from jax import lax
from jax.experimental import pallas as pl
from jax.experimental.pallas import tpu as pltpu
from jax.sharding import PartitionSpec as P

LEV = 127
PADDED = 128
TAPS = 101
HALF = 50
GROUPS = 32
LANES = 128
SIDE = LANES // 2
FIRST = SIDE - HALF
STRIDE = 8
TOGETHER = 4
HIGHEST = lax.Precision.HIGHEST
MESH = pl.DeviceIdType.MESH
OWN, LEFT, RIGHT = 0, 1, 2


def shifted(low, high, lane, amount):
    if amount == 0:
        return low
    return jnp.where(
        lane < LANES - amount,
        pltpu.roll(low, LANES - amount, 1),
        pltpu.roll(high, LANES - amount, 1),
    )


def kernel(
    n_lon,
    n_lat,
    residual_hbm,
    direction_hbm,
    weight_hbm,
    vertical_hbm,
    lon_taps_hbm,
    lat_taps_hbm,
    sizes_hbm,
    image_out,
    alpha_out,
    ratio_out,
    held_w,
    vertical_ref,
    lon_taps_ref,
    lat_taps_ref,
    sizes_ref,
    scales,
    load_sem,
    store_sem,
    held_d,
    held_r,
    held_b,
    matrix,
    flipped,
    gathered,
    gathered_r,
    sides,
    sides_in,
    window,
    shifts,
    lon_coef,
    lat_coef,
    filtered,
    image_part,
    lat_part,
    image,
    sums,
    sums_lat,
    sums_all,
    send_sem,
    recv_sem,
    back_send,
    back_recv,
    lat_send,
    lat_recv,
    lon_send,
    lon_recv,
):
    chunk = PADDED // n_lat
    tiles = chunk // 8
    direct = n_lon * n_lat <= 64
    packed = tiles % 2 == 0
    lane = lax.broadcasted_iota(jnp.int32, (8, LANES), 1)
    my_lon, my_lat = lax.axis_index("lon"), lax.axis_index("lat")
    left = lax.rem(my_lon + n_lon - 1, n_lon)
    right = lax.rem(my_lon + 1, n_lon)

    def lat_at(step):
        return lax.rem(my_lat + step, n_lat)

    def rows_of(index):
        return pl.ds(pl.multiple_of(index * chunk, chunk), chunk)

    def load(source, place, index):
        copy = pltpu.make_async_copy(source, place, load_sem.at[index])
        copy.start()
        return copy

    levels = pl.ds(0, LEV)
    loads = [
        load(direction_hbm.at[:, 0, :], held_d.at[levels, :], 0),
        load(residual_hbm.at[:, 0, :], held_r.at[levels, :], 1),
        load(sizes_hbm, sizes_ref, 2),
        load(lon_taps_hbm, lon_taps_ref, 3),
        load(lat_taps_hbm, lat_taps_ref, 4),
        load(vertical_hbm, vertical_ref, 5),
        load(weight_hbm.at[:, 0, :], held_w.at[levels, :], 6),
    ]

    barrier = pltpu.get_barrier_semaphore()
    greeted = 0
    for step in range(n_lat):
        for lon in (my_lon, left, right):
            if step == 0 and lon is my_lon:
                continue
            pl.semaphore_signal(
                barrier, inc=1, device_id=(lon, lat_at(step)), device_id_type=MESH
            )
            greeted += 1
    for across in range(n_lat if direct else 1):
        for step in range(2, n_lon - 1):
            pl.semaphore_signal(
                barrier,
                inc=1,
                device_id=(lax.rem(my_lon + step, n_lon), lat_at(across)),
                device_id_type=MESH,
            )
            greeted += 1

    held_d[pl.ds(LEV, 1), :] = jnp.zeros((1, LANES), jnp.float32)
    held_r[pl.ds(LEV, 1), :] = jnp.zeros((1, LANES), jnp.float32)
    loads[0].wait()
    loads[1].wait()

    def send_block(held, phase, kind, step):
        to = lat_at(step)
        if packed and kind != OWN:
            return send_side(phase, kind, to)
        lon = (my_lon, left, right)[kind]
        slot = (OWN, RIGHT, LEFT)[kind]
        copy = pltpu.make_async_remote_copy(
            src_ref=held.at[rows_of(to), :],
            dst_ref=gathered.at[phase, slot, my_lat],
            send_sem=send_sem.at[phase, slot, to],
            recv_sem=recv_sem.at[phase, slot, my_lat],
            device_id=(lon, to),
            device_id_type=MESH,
        )
        copy.start()
        return copy

    def send_side(phase, kind, to):
        lon, slot = ((left, 1), (right, 0))[kind - LEFT]
        copy = pltpu.make_async_remote_copy(
            src_ref=sides.at[phase, slot, to],
            dst_ref=sides_in.at[phase, slot, my_lat],
            send_sem=send_sem.at[phase, 1 + slot, to],
            recv_sem=recv_sem.at[phase, 1 + slot, my_lat],
            device_id=(lon, to),
            device_id_type=MESH,
        )
        copy.start()
        return copy

    def pack(held, phase):
        for lat in range(n_lat):
            for at in range(tiles // 2):
                first = held[pl.ds(lat * chunk + at * 8, 8), :]
                second = held[pl.ds(lat * chunk + chunk // 2 + at * 8, 8), :]
                turned = pltpu.roll(first, SIDE, 1)
                row = pl.ds(at * 8, 8)
                sides[phase, 0, lat, row, :] = jnp.where(lane < SIDE, turned, second)
                sides[phase, 1, lat, row, :] = jnp.where(lane < SIDE, second, turned)

    def send_residual(step):
        to = lat_at(step)
        copy = pltpu.make_async_remote_copy(
            src_ref=held_r.at[rows_of(to), :],
            dst_ref=gathered_r.at[my_lat],
            send_sem=send_sem.at[0, 3, to],
            recv_sem=recv_sem.at[0, 3, my_lat],
            device_id=(my_lon, to),
            device_id_type=MESH,
        )
        copy.start()
        return copy

    def arrived(phase, kind, step):
        source = lat_at(step)
        if kind == 3:
            place = gathered_r.at[source]
        elif packed and kind != OWN:
            place = sides_in.at[phase, kind - LEFT, source]
        else:
            place = gathered.at[phase, kind, source]
        pltpu.make_async_remote_copy(
            src_ref=place,
            dst_ref=place,
            send_sem=send_sem.at[phase, kind, source],
            recv_sem=recv_sem.at[phase, kind, source],
            device_id=(my_lon, source),
            device_id_type=MESH,
        ).wait_recv()

    def send_all(held, phase):
        copies = []
        for step in list(range(1, n_lat)) + [0]:
            for kind in (LEFT, RIGHT, OWN):
                if step or kind:
                    copies.append(send_block(held, phase, kind, step))
        gathered[phase, OWN, my_lat] = held[rows_of(my_lat), :]
        return copies

    def await_all(phase):
        for step in range(n_lat):
            for kind in (OWN, LEFT, RIGHT):
                if step or kind:
                    arrived(phase, kind, step)

    def send_back(parts, whole, phase):
        copies = []
        for step in range(1, n_lat):
            to = lat_at(step)
            copy = pltpu.make_async_remote_copy(
                src_ref=parts.at[to],
                dst_ref=whole.at[rows_of(my_lat), :],
                send_sem=back_send.at[phase, to],
                recv_sem=back_recv.at[phase, my_lat],
                device_id=(my_lon, to),
                device_id_type=MESH,
            )
            copy.start()
            copies.append(copy)
        whole[rows_of(my_lat), :] = parts[my_lat]
        return copies

    def await_back(whole, phase):
        for step in range(1, n_lat):
            source = lat_at(step)
            place = whole.at[rows_of(source), :]
            pltpu.make_async_remote_copy(
                src_ref=place,
                dst_ref=place,
                send_sem=back_send.at[phase, source],
                recv_sem=back_recv.at[phase, source],
                device_id=(my_lon, source),
                device_id_type=MESH,
            ).wait_recv()

    if packed:
        pack(held_d, 0)
    pl.semaphore_wait(barrier, greeted)
    pending = send_all(held_d, 0)
    gathered_r[my_lat] = held_r[rows_of(my_lat), :]

    for copy in loads[2:6]:
        copy.wait()

    upto = (
        lax.broadcasted_iota(jnp.int32, (GROUPS, GROUPS), 0)
        <= lax.broadcasted_iota(jnp.int32, (GROUPS, GROUPS), 1)
    ).astype(jnp.float32)
    sizes = jnp.broadcast_to(sizes_ref[...].astype(jnp.float32), (8, GROUPS))
    bounds = jnp.dot(sizes, upto, precision=HIGHEST)[0:1, :]
    starts = bounds - sizes[0:1, :]
    level = (
        lax.broadcasted_iota(jnp.int32, (chunk, GROUPS), 0) + my_lat * chunk
    ).astype(jnp.float32)
    member = ((level > starts - 0.5) & (level < bounds - 0.5)).astype(jnp.float32)
    lon_rows = jnp.dot(member, lon_taps_ref[...], precision=HIGHEST)
    lat_rows = jnp.dot(member, lat_taps_ref[...], precision=HIGHEST)
    for tap in range(TAPS):
        lon_coef[tap] = jnp.broadcast_to(lon_rows[:, tap : tap + 1], (chunk, LANES))
    for offset in range(2 * n_lat - 1):
        tap = HALF - (n_lat - 1) + offset
        if 0 <= tap < TAPS:
            lat_coef[offset] = jnp.broadcast_to(lat_rows[:, tap : tap + 1], (chunk, LANES))
        else:
            lat_coef[offset] = jnp.zeros((chunk, LANES), jnp.float32)

    matrix[...] = jnp.zeros_like(matrix)
    matrix[pl.ds(0, LEV), pl.ds(0, LEV)] = vertical_ref[...]
    flipped[...] = matrix[...].T


    def filter_chunk(phase, adjoint, finish):
        for at in range(tiles):
            row = pl.ds(at * 8, 8)
            for lat in range(n_lat):
                mine = pltpu.roll(gathered[phase, OWN, lat, row, :], SIDE, 1)
                if packed:
                    half = pl.ds(at % (tiles // 2) * 8, 8)
                    before = sides_in[phase, 0, lat, half, :]
                    after = sides_in[phase, 1, lat, half, :]
                else:
                    before = gathered[phase, LEFT, lat, row, :]
                    after = gathered[phase, RIGHT, lat, row, :]
                if not packed or at >= tiles // 2:
                    before = pltpu.roll(before, SIDE, 1)
                    after = pltpu.roll(after, SIDE, 1)
                window[lat, 0, row, :] = jnp.where(lane < SIDE, before, mine)
                window[lat, 1, row, :] = jnp.where(lane < SIDE, mine, after)

        def some(at, _):
            first = lax.rem(at, n_lat // TOGETHER) * TOGETHER
            row = pl.ds(pl.multiple_of(at // (n_lat // TOGETHER) * 8, 8), 8)
            for out in range(TOGETHER):
                low = jnp.zeros((8, LANES), jnp.float32)
                high = jnp.zeros((8, LANES), jnp.float32)
                for lat in range(n_lat):
                    offset = first + (out - lat) if adjoint else lat - out - first
                    scale = lat_coef[offset + n_lat - 1, row, :]
                    low = low + scale * window[lat, 0, row, :]
                    high = high + scale * window[lat, 1, row, :]
                for j in range(STRIDE):
                    shifts[out, 0, j] = shifted(low, high, lane, j)
                    shifts[out, 1, j] = shifted(high, low, lane, j)
            totals = [jnp.zeros((8, LANES), jnp.float32)] * TOGETHER
            for base in range(0, TAPS, STRIDE):
                parts = [None] * TOGETHER
                for j in range(min(STRIDE, TAPS - base)):
                    tap = base + j
                    scale = lon_coef[TAPS - 1 - tap if adjoint else tap, row, :]
                    for out in range(TOGETHER):
                        low, high = scale * shifts[out, 0, j], scale * shifts[out, 1, j]
                        if parts[out] is not None:
                            low, high = parts[out][0] + low, parts[out][1] + high
                        parts[out] = low, high
                for out in range(TOGETHER):
                    totals[out] = totals[out] + shifted(*parts[out], lane, FIRST + base)
            for out in range(TOGETHER):
                finish(first + out, row, totals[out])
            return 0

        lax.fori_loop(0, tiles * (n_lat // TOGETHER), some, 0)

    loads[6].wait()
    await_all(0)

    pending += [send_residual(step) for step in range(1, n_lat)]

    def keep(out_lat, row, total):
        filtered[out_lat, row, :] = total

    filter_chunk(0, False, keep)
    pending += send_back(filtered, lat_part, 0)
    await_back(lat_part, 0)

    lifted = jnp.dot(matrix[...], lat_part[...], precision=HIGHEST)
    held_b[...] = lifted
    held_b[pl.ds(0, LEV), :] = held_b[pl.ds(0, LEV), :] * held_w[levels, :]
    held_b[...] = jnp.dot(flipped[...], held_b[...], precision=HIGHEST)

    if packed:
        pack(held_b, 1)
    pending += send_all(held_b, 1)
    for step in range(1, n_lat):
        arrived(0, 3, step)
    await_all(1)

    sums[...] = jnp.zeros_like(sums)

    def add(out_lat, row, total):
        total = total + gathered[0, OWN, out_lat, row, :]
        image_part[out_lat, row, :] = total
        old = gathered_r[out_lat, row, :]
        sums[0] += old * old
        sums[1] += total * gathered[0, OWN, out_lat, row, :]
        sums[2] += total * old
        sums[3] += total * total

    filter_chunk(1, True, add)
    pending += send_back(image_part, image, 1)

    def exchange(slots, send, recv, mine, count, to_device, between=lambda: None):
        copies = []
        for step in range(1, count):
            to = lax.rem(mine + step, count)
            copy = pltpu.make_async_remote_copy(
                src_ref=slots.at[mine],
                dst_ref=slots.at[mine],
                send_sem=send.at[to],
                recv_sem=recv.at[mine],
                device_id=to_device(to),
                device_id_type=MESH,
            )
            copy.start()
            copies.append(copy)
        between()
        for step in range(1, count):
            source = lax.rem(mine + step, count)
            pltpu.make_async_remote_copy(
                src_ref=slots.at[source],
                dst_ref=slots.at[source],
                send_sem=send.at[source],
                recv_sem=recv.at[source],
                device_id=to_device(source),
                device_id_type=MESH,
            ).wait_recv()
        total = slots[0]
        for index in range(1, count):
            total = total + slots[index]
        return total, copies

    store = pltpu.make_async_copy(
        image.at[levels, :], image_out.at[:, 0, :], store_sem.at[0]
    )

    def put_image():
        await_back(image, 1)
        store.start()

    rows = [jnp.sum(sums[i], axis=0, keepdims=True) for i in range(4)]
    mine = jnp.concatenate(rows + [jnp.zeros((4, LANES), jnp.float32)], axis=0)
    if direct:
        me = my_lon * n_lat + my_lat
        sums_all[me] = mine
        total, copies = exchange(
            sums_all,
            lon_send,
            lon_recv,
            me,
            n_lon * n_lat,
            lambda to: (to // n_lat, lax.rem(to, n_lat)),
            put_image,
        )
        pending += copies
    else:
        sums_lat[my_lat] = mine
        total, copies = exchange(
            sums_lat, lat_send, lat_recv, my_lat, n_lat, lambda to: (my_lon, to)
        )
        pending += copies
        sums_all[my_lon] = total
        total, copies = exchange(
            sums_all, lon_send, lon_recv, my_lon, n_lon, lambda to: (to, my_lat), put_image
        )
        pending += copies
    total = jnp.sum(total, axis=1, keepdims=True)
    norm_old, curvature = total[0:1, :], total[1:2, :]
    crossed, squared = total[2:3, :], total[3:4, :]
    alpha = norm_old / curvature
    norm_new = norm_old - 2.0 * alpha * crossed + alpha * alpha * squared
    ratio = norm_new / norm_old
    scales[0] = jnp.broadcast_to(alpha, (1, LANES))
    scales[1] = jnp.broadcast_to(ratio, (1, LANES))
    stores = [store]
    for index, out in enumerate((alpha_out, ratio_out)):
        copy = pltpu.make_async_copy(
            scales.at[pl.ds(index, 1)], out, store_sem.at[1 + index]
        )
        copy.start()
        stores.append(copy)

    for copy in pending:
        copy.wait_send()
    for copy in stores:
        copy.wait()


def local(n_lon, n_lat, iterate, residual, direction, obs_weight, vertical, lon_taps, lat_taps, band_sizes):
    chunk = PADDED // n_lat
    last = n_lon * n_lat if n_lon * n_lat <= 64 else n_lon
    f32 = jnp.float32
    side_shape = (2, 2, n_lat, max(8, chunk // 2), LANES)
    hbm = pl.BlockSpec(memory_space=pltpu.HBM)
    image, alpha, ratio = pl.pallas_call(
        functools.partial(kernel, n_lon, n_lat),
        out_shape=[
            jax.ShapeDtypeStruct((LEV, 1, LANES), f32),
            jax.ShapeDtypeStruct((1, 1, LANES), f32),
            jax.ShapeDtypeStruct((1, 1, LANES), f32),
        ],
        in_specs=[hbm] * 7,
        out_specs=[hbm] * 3,
        scratch_shapes=[
            pltpu.VMEM((PADDED, LANES), f32),
            pltpu.VMEM((LEV, LEV), f32),
            pltpu.VMEM((GROUPS, TAPS), f32),
            pltpu.VMEM((GROUPS, TAPS), f32),
            pltpu.VMEM((1, GROUPS), jnp.int32),
            pltpu.VMEM((2, 1, LANES), f32),
            pltpu.SemaphoreType.DMA((7,)),
            pltpu.SemaphoreType.DMA((3,)),
            pltpu.VMEM((PADDED, LANES), f32),
            pltpu.VMEM((PADDED, LANES), f32),
            pltpu.VMEM((PADDED, LANES), f32),
            pltpu.VMEM((PADDED, PADDED), f32),
            pltpu.VMEM((PADDED, PADDED), f32),
            pltpu.VMEM((2, 3, n_lat, chunk, LANES), f32),
            pltpu.VMEM((n_lat, chunk, LANES), f32),
            pltpu.VMEM(side_shape, f32),
            pltpu.VMEM(side_shape, f32),
            pltpu.VMEM((n_lat, 2, chunk, LANES), f32),
            pltpu.VMEM((TOGETHER, 2, STRIDE, 8, LANES), f32),
            pltpu.VMEM((TAPS, chunk, LANES), f32),
            pltpu.VMEM((2 * n_lat - 1, chunk, LANES), f32),
            pltpu.VMEM((n_lat, chunk, LANES), f32),
            pltpu.VMEM((n_lat, chunk, LANES), f32),
            pltpu.VMEM((PADDED, LANES), f32),
            pltpu.VMEM((PADDED, LANES), f32),
            pltpu.VMEM((4, 8, LANES), f32),
            pltpu.VMEM((n_lat, 8, LANES), f32),
            pltpu.VMEM((last, 8, LANES), f32),
            pltpu.SemaphoreType.DMA((2, 4, n_lat)),
            pltpu.SemaphoreType.DMA((2, 4, n_lat)),
            pltpu.SemaphoreType.DMA((2, n_lat)),
            pltpu.SemaphoreType.DMA((2, n_lat)),
            pltpu.SemaphoreType.DMA((n_lat,)),
            pltpu.SemaphoreType.DMA((n_lat,)),
            pltpu.SemaphoreType.DMA((last,)),
            pltpu.SemaphoreType.DMA((last,)),
        ],
        compiler_params=pltpu.CompilerParams(
            collective_id=0,
            has_side_effects=True,
            vmem_limit_bytes=64 * 1024 * 1024,
        ),
    )(
        residual,
        direction,
        obs_weight,
        vertical,
        lon_taps,
        lat_taps,
        band_sizes.reshape(1, GROUPS),
    )
    residual_next = residual - alpha * image
    return (
        iterate + alpha * direction,
        residual_next,
        residual_next + ratio * direction,
    )


def solution(mesh):
    field = P(None, "lat", "lon")
    return jax.shard_map(
        functools.partial(local, mesh.shape["lon"], mesh.shape["lat"]),
        mesh=mesh,
        in_specs=(field,) * 4 + (P(),) * 4,
        out_specs=(field,) * 3,
        check_vma=False,
    )
```

```python
import functools

import jax
import jax.numpy as jnp
from jax import lax
from jax.experimental import pallas as pl
from jax.experimental.pallas import tpu as pltpu
from jax.sharding import PartitionSpec as P

LEV = 127
PADDED = 128
TAPS = 101
HALF = 50
GROUPS = 32
LANES = 128
SIDE = LANES // 2
FIRST = SIDE - HALF
STRIDE = 8
TOGETHER = 4
HIGHEST = lax.Precision.HIGHEST
MESH = pl.DeviceIdType.MESH
OWN, LEFT, RIGHT = 0, 1, 2


def shifted(low, high, lane, amount):
    if amount == 0:
        return low
    return jnp.where(
        lane < LANES - amount,
        pltpu.roll(low, LANES - amount, 1),
        pltpu.roll(high, LANES - amount, 1),
    )


def kernel(
    n_lon,
    n_lat,
    residual_hbm,
    direction_hbm,
    weight_hbm,
    vertical_hbm,
    lon_taps_hbm,
    lat_taps_hbm,
    sizes_hbm,
    image_out,
    alpha_out,
    ratio_out,
    held_w,
    vertical_ref,
    lon_taps_ref,
    lat_taps_ref,
    sizes_ref,
    scales,
    load_sem,
    store_sem,
    held_d,
    held_r,
    held_b,
    matrix,
    flipped,
    gathered,
    gathered_r,
    sides,
    sides_in,
    window,
    shifts,
    lon_coef,
    lat_coef,
    filtered,
    image_part,
    lat_part,
    image,
    sums,
    sums_lat,
    sums_all,
    send_sem,
    recv_sem,
    back_send,
    back_recv,
    lat_send,
    lat_recv,
    lon_send,
    lon_recv,
):
    chunk = PADDED // n_lat
    tiles = chunk // 8
    direct = n_lon * n_lat <= 64
    packed = tiles % 2 == 0
    lane = lax.broadcasted_iota(jnp.int32, (8, LANES), 1)
    my_lon, my_lat = lax.axis_index("lon"), lax.axis_index("lat")
    left = lax.rem(my_lon + n_lon - 1, n_lon)
    right = lax.rem(my_lon + 1, n_lon)

    def lat_at(step):
        return lax.rem(my_lat + step, n_lat)

    def rows_of(index):
        return pl.ds(pl.multiple_of(index * chunk, chunk), chunk)

    def load(source, place, index):
        copy = pltpu.make_async_copy(source, place, load_sem.at[index])
        copy.start()
        return copy

    levels = pl.ds(0, LEV)
    loads = [
        load(direction_hbm.at[:, 0, :], held_d.at[levels, :], 0),
        load(residual_hbm.at[:, 0, :], held_r.at[levels, :], 1),
        load(sizes_hbm, sizes_ref, 2),
        load(lon_taps_hbm, lon_taps_ref, 3),
        load(lat_taps_hbm, lat_taps_ref, 4),
        load(vertical_hbm, vertical_ref, 5),
        load(weight_hbm.at[:, 0, :], held_w.at[levels, :], 6),
    ]

    barrier = pltpu.get_barrier_semaphore()
    greeted = 0
    for step in range(n_lat):
        for lon in (my_lon, left, right):
            if step == 0 and lon is my_lon:
                continue
            pl.semaphore_signal(
                barrier, inc=1, device_id=(lon, lat_at(step)), device_id_type=MESH
            )
            greeted += 1
    for across in range(n_lat if direct else 1):
        for step in range(2, n_lon - 1):
            pl.semaphore_signal(
                barrier,
                inc=1,
                device_id=(lax.rem(my_lon + step, n_lon), lat_at(across)),
                device_id_type=MESH,
            )
            greeted += 1

    held_d[pl.ds(LEV, 1), :] = jnp.zeros((1, LANES), jnp.float32)
    held_r[pl.ds(LEV, 1), :] = jnp.zeros((1, LANES), jnp.float32)
    loads[0].wait()
    loads[1].wait()

    def send_block(held, phase, kind, step):
        to = lat_at(step)
        if packed and kind != OWN:
            return send_side(phase, kind, to)
        lon = (my_lon, left, right)[kind]
        slot = (OWN, RIGHT, LEFT)[kind]
        copy = pltpu.make_async_remote_copy(
            src_ref=held.at[rows_of(to), :],
            dst_ref=gathered.at[phase, slot, my_lat],
            send_sem=send_sem.at[phase, slot, to],
            recv_sem=recv_sem.at[phase, slot, my_lat],
            device_id=(lon, to),
            device_id_type=MESH,
        )
        copy.start()
        return copy

    def send_side(phase, kind, to):
        lon, slot = ((left, 1), (right, 0))[kind - LEFT]
        copy = pltpu.make_async_remote_copy(
            src_ref=sides.at[phase, slot, to],
            dst_ref=sides_in.at[phase, slot, my_lat],
            send_sem=send_sem.at[phase, 1 + slot, to],
            recv_sem=recv_sem.at[phase, 1 + slot, my_lat],
            device_id=(lon, to),
            device_id_type=MESH,
        )
        copy.start()
        return copy

    def pack(held, phase):
        for lat in range(n_lat):
            for at in range(tiles // 2):
                first = held[pl.ds(lat * chunk + at * 8, 8), :]
                second = held[pl.ds(lat * chunk + chunk // 2 + at * 8, 8), :]
                turned = pltpu.roll(first, SIDE, 1)
                row = pl.ds(at * 8, 8)
                sides[phase, 0, lat, row, :] = jnp.where(lane < SIDE, turned, second)
                sides[phase, 1, lat, row, :] = jnp.where(lane < SIDE, second, turned)

    def send_residual(step):
        to = lat_at(step)
        copy = pltpu.make_async_remote_copy(
            src_ref=held_r.at[rows_of(to), :],
            dst_ref=gathered_r.at[my_lat],
            send_sem=send_sem.at[0, 3, to],
            recv_sem=recv_sem.at[0, 3, my_lat],
            device_id=(my_lon, to),
            device_id_type=MESH,
        )
        copy.start()
        return copy

    def arrived(phase, kind, step):
        source = lat_at(step)
        if kind == 3:
            place = gathered_r.at[source]
        elif packed and kind != OWN:
            place = sides_in.at[phase, kind - LEFT, source]
        else:
            place = gathered.at[phase, kind, source]
        pltpu.make_async_remote_copy(
            src_ref=place,
            dst_ref=place,
            send_sem=send_sem.at[phase, kind, source],
            recv_sem=recv_sem.at[phase, kind, source],
            device_id=(my_lon, source),
            device_id_type=MESH,
        ).wait_recv()

    def send_all(held, phase):
        copies = []
        for step in list(range(1, n_lat)) + [0]:
            for kind in (LEFT, RIGHT, OWN):
                if step or kind:
                    copies.append(send_block(held, phase, kind, step))
        gathered[phase, OWN, my_lat] = held[rows_of(my_lat), :]
        return copies

    def await_all(phase):
        for step in range(n_lat):
            for kind in (OWN, LEFT, RIGHT):
                if step or kind:
                    arrived(phase, kind, step)

    def send_back(parts, whole, phase):
        copies = []
        for step in range(1, n_lat):
            to = lat_at(step)
            copy = pltpu.make_async_remote_copy(
                src_ref=parts.at[to],
                dst_ref=whole.at[rows_of(my_lat), :],
                send_sem=back_send.at[phase, to],
                recv_sem=back_recv.at[phase, my_lat],
                device_id=(my_lon, to),
                device_id_type=MESH,
            )
            copy.start()
            copies.append(copy)
        whole[rows_of(my_lat), :] = parts[my_lat]
        return copies

    def await_back(whole, phase):
        for step in range(1, n_lat):
            source = lat_at(step)
            place = whole.at[rows_of(source), :]
            pltpu.make_async_remote_copy(
                src_ref=place,
                dst_ref=place,
                send_sem=back_send.at[phase, source],
                recv_sem=back_recv.at[phase, source],
                device_id=(my_lon, source),
                device_id_type=MESH,
            ).wait_recv()

    if packed:
        pack(held_d, 0)
    pl.semaphore_wait(barrier, greeted)
    pending = send_all(held_d, 0)
    gathered_r[my_lat] = held_r[rows_of(my_lat), :]

    for copy in loads[2:6]:
        copy.wait()

    upto = (
        lax.broadcasted_iota(jnp.int32, (GROUPS, GROUPS), 0)
        <= lax.broadcasted_iota(jnp.int32, (GROUPS, GROUPS), 1)
    ).astype(jnp.float32)
    sizes = jnp.broadcast_to(sizes_ref[...].astype(jnp.float32), (8, GROUPS))
    bounds = jnp.dot(sizes, upto, precision=HIGHEST)[0:1, :]
    starts = bounds - sizes[0:1, :]
    level = (
        lax.broadcasted_iota(jnp.int32, (chunk, GROUPS), 0) + my_lat * chunk
    ).astype(jnp.float32)
    member = ((level > starts - 0.5) & (level < bounds - 0.5)).astype(jnp.float32)
    lon_rows = jnp.dot(member, lon_taps_ref[...], precision=HIGHEST)
    lat_rows = jnp.dot(member, lat_taps_ref[...], precision=HIGHEST)
    for tap in range(TAPS):
        lon_coef[tap] = jnp.broadcast_to(lon_rows[:, tap : tap + 1], (chunk, LANES))
    for offset in range(2 * n_lat - 1):
        tap = HALF - (n_lat - 1) + offset
        if 0 <= tap < TAPS:
            lat_coef[offset] = jnp.broadcast_to(lat_rows[:, tap : tap + 1], (chunk, LANES))
        else:
            lat_coef[offset] = jnp.zeros((chunk, LANES), jnp.float32)

    matrix[...] = jnp.zeros_like(matrix)
    matrix[pl.ds(0, LEV), pl.ds(0, LEV)] = vertical_ref[...]
    flipped[...] = matrix[...].T


    def filter_chunk(phase, adjoint, finish):
        for at in range(tiles):
            row = pl.ds(at * 8, 8)
            for lat in range(n_lat):
                mine = pltpu.roll(gathered[phase, OWN, lat, row, :], SIDE, 1)
                if packed:
                    half = pl.ds(at % (tiles // 2) * 8, 8)
                    before = sides_in[phase, 0, lat, half, :]
                    after = sides_in[phase, 1, lat, half, :]
                else:
                    before = gathered[phase, LEFT, lat, row, :]
                    after = gathered[phase, RIGHT, lat, row, :]
                if not packed or at >= tiles // 2:
                    before = pltpu.roll(before, SIDE, 1)
                    after = pltpu.roll(after, SIDE, 1)
                window[lat, 0, row, :] = jnp.where(lane < SIDE, before, mine)
                window[lat, 1, row, :] = jnp.where(lane < SIDE, mine, after)

        def some(at, _):
            first = lax.rem(at, n_lat // TOGETHER) * TOGETHER
            row = pl.ds(pl.multiple_of(at // (n_lat // TOGETHER) * 8, 8), 8)
            for out in range(TOGETHER):
                low = jnp.zeros((8, LANES), jnp.float32)
                high = jnp.zeros((8, LANES), jnp.float32)
                for lat in range(n_lat):
                    offset = first + (out - lat) if adjoint else lat - out - first
                    scale = lat_coef[offset + n_lat - 1, row, :]
                    low = low + scale * window[lat, 0, row, :]
                    high = high + scale * window[lat, 1, row, :]
                for j in range(STRIDE):
                    shifts[out, 0, j] = shifted(low, high, lane, j)
                    shifts[out, 1, j] = shifted(high, low, lane, j)
            totals = [jnp.zeros((8, LANES), jnp.float32)] * TOGETHER
            for base in range(0, TAPS, STRIDE):
                parts = [None] * TOGETHER
                for j in range(min(STRIDE, TAPS - base)):
                    tap = base + j
                    scale = lon_coef[TAPS - 1 - tap if adjoint else tap, row, :]
                    for out in range(TOGETHER):
                        low, high = scale * shifts[out, 0, j], scale * shifts[out, 1, j]
                        if parts[out] is not None:
                            low, high = parts[out][0] + low, parts[out][1] + high
                        parts[out] = low, high
                for out in range(TOGETHER):
                    totals[out] = totals[out] + shifted(*parts[out], lane, FIRST + base)
            for out in range(TOGETHER):
                finish(first + out, row, totals[out])
            return 0

        lax.fori_loop(0, tiles * (n_lat // TOGETHER), some, 0)

    loads[6].wait()
    await_all(0)

    pending += [send_residual(step) for step in range(1, n_lat)]

    def keep(out_lat, row, total):
        filtered[out_lat, row, :] = total

    filter_chunk(0, False, keep)
    pending += send_back(filtered, lat_part, 0)
    await_back(lat_part, 0)

    lifted = jnp.dot(matrix[...], lat_part[...], precision=HIGHEST)
    held_b[...] = lifted
    held_b[pl.ds(0, LEV), :] = held_b[pl.ds(0, LEV), :] * held_w[levels, :]
    held_b[...] = jnp.dot(flipped[...], held_b[...], precision=HIGHEST)

    if packed:
        pack(held_b, 1)
    pending += send_all(held_b, 1)
    for step in range(1, n_lat):
        arrived(0, 3, step)
    await_all(1)

    sums[...] = jnp.zeros_like(sums)

    def add(out_lat, row, total):
        total = total + gathered[0, OWN, out_lat, row, :]
        image_part[out_lat, row, :] = total
        old = gathered_r[out_lat, row, :]
        sums[0] += old * old
        sums[1] += total * gathered[0, OWN, out_lat, row, :]
        sums[2] += total * old
        sums[3] += total * total

    filter_chunk(1, True, add)

    def exchange(slots, send, recv, mine, count, to_device, between=lambda: None):
        copies = []
        for step in range(1, count):
            to = lax.rem(mine + step, count)
            copy = pltpu.make_async_remote_copy(
                src_ref=slots.at[mine],
                dst_ref=slots.at[mine],
                send_sem=send.at[to],
                recv_sem=recv.at[mine],
                device_id=to_device(to),
                device_id_type=MESH,
            )
            copy.start()
            copies.append(copy)
        between()
        for step in range(1, count):
            source = lax.rem(mine + step, count)
            pltpu.make_async_remote_copy(
                src_ref=slots.at[source],
                dst_ref=slots.at[source],
                send_sem=send.at[source],
                recv_sem=recv.at[source],
                device_id=to_device(source),
                device_id_type=MESH,
            ).wait_recv()
        total = slots[0]
        for index in range(1, count):
            total = total + slots[index]
        return total, copies

    store = pltpu.make_async_copy(
        image.at[levels, :], image_out.at[:, 0, :], store_sem.at[0]
    )

    def put_image():
        pending.extend(send_back(image_part, image, 1))
        await_back(image, 1)
        store.start()

    rows = [jnp.sum(sums[i], axis=0, keepdims=True) for i in range(4)]
    mine = jnp.concatenate(rows + [jnp.zeros((4, LANES), jnp.float32)], axis=0)
    if direct:
        me = my_lon * n_lat + my_lat
        sums_all[me] = mine
        total, copies = exchange(
            sums_all,
            lon_send,
            lon_recv,
            me,
            n_lon * n_lat,
            lambda to: (to // n_lat, lax.rem(to, n_lat)),
            put_image,
        )
        pending += copies
    else:
        sums_lat[my_lat] = mine
        total, copies = exchange(
            sums_lat, lat_send, lat_recv, my_lat, n_lat, lambda to: (my_lon, to)
        )
        pending += copies
        sums_all[my_lon] = total
        total, copies = exchange(
            sums_all, lon_send, lon_recv, my_lon, n_lon, lambda to: (to, my_lat), put_image
        )
        pending += copies
    total = jnp.sum(total, axis=1, keepdims=True)
    norm_old, curvature = total[0:1, :], total[1:2, :]
    crossed, squared = total[2:3, :], total[3:4, :]
    alpha = norm_old / curvature
    norm_new = norm_old - 2.0 * alpha * crossed + alpha * alpha * squared
    ratio = norm_new / norm_old
    scales[0] = jnp.broadcast_to(alpha, (1, LANES))
    scales[1] = jnp.broadcast_to(ratio, (1, LANES))
    stores = [store]
    for index, out in enumerate((alpha_out, ratio_out)):
        copy = pltpu.make_async_copy(
            scales.at[pl.ds(index, 1)], out, store_sem.at[1 + index]
        )
        copy.start()
        stores.append(copy)

    for copy in pending:
        copy.wait_send()
    for copy in stores:
        copy.wait()


def local(n_lon, n_lat, iterate, residual, direction, obs_weight, vertical, lon_taps, lat_taps, band_sizes):
    chunk = PADDED // n_lat
    last = n_lon * n_lat if n_lon * n_lat <= 64 else n_lon
    f32 = jnp.float32
    side_shape = (2, 2, n_lat, max(8, chunk // 2), LANES)
    hbm = pl.BlockSpec(memory_space=pltpu.HBM)
    image, alpha, ratio = pl.pallas_call(
        functools.partial(kernel, n_lon, n_lat),
        out_shape=[
            jax.ShapeDtypeStruct((LEV, 1, LANES), f32),
            jax.ShapeDtypeStruct((1, 1, LANES), f32),
            jax.ShapeDtypeStruct((1, 1, LANES), f32),
        ],
        in_specs=[hbm] * 7,
        out_specs=[hbm] * 3,
        scratch_shapes=[
            pltpu.VMEM((PADDED, LANES), f32),
            pltpu.VMEM((LEV, LEV), f32),
            pltpu.VMEM((GROUPS, TAPS), f32),
            pltpu.VMEM((GROUPS, TAPS), f32),
            pltpu.VMEM((1, GROUPS), jnp.int32),
            pltpu.VMEM((2, 1, LANES), f32),
            pltpu.SemaphoreType.DMA((7,)),
            pltpu.SemaphoreType.DMA((3,)),
            pltpu.VMEM((PADDED, LANES), f32),
            pltpu.VMEM((PADDED, LANES), f32),
            pltpu.VMEM((PADDED, LANES), f32),
            pltpu.VMEM((PADDED, PADDED), f32),
            pltpu.VMEM((PADDED, PADDED), f32),
            pltpu.VMEM((2, 3, n_lat, chunk, LANES), f32),
            pltpu.VMEM((n_lat, chunk, LANES), f32),
            pltpu.VMEM(side_shape, f32),
            pltpu.VMEM(side_shape, f32),
            pltpu.VMEM((n_lat, 2, chunk, LANES), f32),
            pltpu.VMEM((TOGETHER, 2, STRIDE, 8, LANES), f32),
            pltpu.VMEM((TAPS, chunk, LANES), f32),
            pltpu.VMEM((2 * n_lat - 1, chunk, LANES), f32),
            pltpu.VMEM((n_lat, chunk, LANES), f32),
            pltpu.VMEM((n_lat, chunk, LANES), f32),
            pltpu.VMEM((PADDED, LANES), f32),
            pltpu.VMEM((PADDED, LANES), f32),
            pltpu.VMEM((4, 8, LANES), f32),
            pltpu.VMEM((n_lat, 8, LANES), f32),
            pltpu.VMEM((last, 8, LANES), f32),
            pltpu.SemaphoreType.DMA((2, 4, n_lat)),
            pltpu.SemaphoreType.DMA((2, 4, n_lat)),
            pltpu.SemaphoreType.DMA((2, n_lat)),
            pltpu.SemaphoreType.DMA((2, n_lat)),
            pltpu.SemaphoreType.DMA((n_lat,)),
            pltpu.SemaphoreType.DMA((n_lat,)),
            pltpu.SemaphoreType.DMA((last,)),
            pltpu.SemaphoreType.DMA((last,)),
        ],
        compiler_params=pltpu.CompilerParams(
            collective_id=0,
            has_side_effects=True,
            vmem_limit_bytes=64 * 1024 * 1024,
        ),
    )(
        residual,
        direction,
        obs_weight,
        vertical,
        lon_taps,
        lat_taps,
        band_sizes.reshape(1, GROUPS),
    )
    residual_next = residual - alpha * image
    return (
        iterate + alpha * direction,
        residual_next,
        residual_next + ratio * direction,
    )


def solution(mesh):
    field = P(None, "lat", "lon")
    return jax.shard_map(
        functools.partial(local, mesh.shape["lon"], mesh.shape["lat"]),
        mesh=mesh,
        in_specs=(field,) * 4 + (P(),) * 4,
        out_specs=(field,) * 3,
        check_vma=False,
    )
```
